256 devices in a mesh: replica: 32 (over y, x, core), tensor: 8 (over z).
Axes of the slice: x: 4, y: 4, z: 8, core: 2. Of those that a mesh axis runs over, the one named last changes fastest.
Arguments:
- x_rows: bfloat16 [4096, 8192], P('replica', 'tensor'), may hold values from -6 to 6
- v_weight: bfloat16 [8192, 1024], P(None, 'tensor'), may hold values from -0.0625 to 0.0625
- home_a: bfloat16 [512, 64, 8192], P('replica', None, 'tensor'), may hold values from -0.0625 to 0.0625
- home_b: bfloat16 [512, 64, 1024], P('replica', None, 'tensor'), may hold values from -0.75 to 0.75
- cache_a: bfloat16 [1536, 64, 8192], P('replica', None, 'tensor'), may hold values from -0.0625 to 0.0625
- cache_b: bfloat16 [1536, 64, 1024], P('replica', None, 'tensor'), may hold values from -0.75 to 0.75
- miss_ids: int32 [32, 32], P('replica'), may hold values from 0 to 511, as said below
- evict_slots: int32 [32, 32], P('replica'), may hold values from 0 to 47, as said below
- slot_ids: int32 [32, 48], P('replica'), may hold values from 0 to 511, as said below
- row_ids: int32 [4096], P('replica'), may hold values from 0 to 511, as said below
Outputs:
- value_out: bfloat16 [4096, 1024], P('replica', 'tensor')
The draws below stay inside these ranges and needn't reach their ends.
Inputs may be any that keep to these rules, and one draw needn't show every extreme that they name: `miss_ids`: each replica's 32 ids are distinct and none is homed on the replica itself; at most 2 are homed on any one replica, and exactly 2 on some replica in every list. `evict_slots`: each replica's entries are distinct slots. `slot_ids`: the slots that are not evicted hold the 16 adapters homed on the replica itself, each once; evicted slots hold arbitrary ids. `row_ids`: every row names an adapter that its replica holds after the evicted slots are refilled.
All inputs are finite; a program needn't handle non-finite values.
Results may differ from the reference program's by a relative error of at most 0.0046.
Values may be sent and summed in bfloat16 or wider, within the bound.
No kernel may reach another device: no remote copies, remote signals or barrier semaphores. Data moves between devices by JAX's collectives and lax.ppermute only.
A program may use at most 128 MiB of HBM per device.

```python
import jax
import jax.numpy as jnp
from jax import lax

D = 8192
VW = 1024
R = 64
ROWS = 128
ADP_DEV = 16
MISS = 32
CAP = 2
CACHE = 48
REPLICAS = 32
ADAPTERS = 512
TOKENS = 4096


def plan_lists(key):

    def one_replica(replica):
        branch = jax.random.fold_in(key, replica)
        keys = jax.random.split(branch, 7)
        others = (replica + 1 + jnp.arange(REPLICAS - 1, dtype=jnp.int32)) % REPLICAS
        first = jax.random.randint(keys[0], (), 0, REPLICAS - 1)
        pair_home = jnp.repeat(others, CAP)
        pair_order = jnp.tile(jnp.arange(CAP, dtype=jnp.int32), REPLICAS - 1)
        scores = jax.random.permutation(keys[1], (REPLICAS - 1) * CAP).astype(jnp.int32)
        scores = jnp.where(pair_home == others[first], -1 - pair_order, scores)
        picked = jnp.argsort(scores)[:MISS]
        chosen_home = pair_home[picked]
        chosen_order = pair_order[picked]
        inner = jax.vmap(lambda sub: jax.random.permutation(sub, ADP_DEV))(jax.random.split(keys[2], REPLICAS)).astype(jnp.int32)
        wanted = chosen_home * ADP_DEV + inner[chosen_home, chosen_order]
        wanted = jax.random.permutation(keys[3], wanted).astype(jnp.int32)
        slots = jax.random.permutation(keys[4], CACHE).astype(jnp.int32)
        evicted = slots[:MISS]
        kept = slots[MISS:]
        table = jnp.zeros((CACHE,), jnp.int32).at[kept].set(replica * ADP_DEV + jnp.arange(ADP_DEV, dtype=jnp.int32))
        table = table.at[evicted].set(wanted)
        stale = jax.random.randint(keys[5], (MISS,), 0, ADAPTERS).astype(jnp.int32)
        before = table.at[evicted].set(stale)
        pick = jax.random.randint(keys[6], (ROWS,), 0, CACHE)
        return (wanted, evicted, before, table[pick])
    return jax.vmap(one_replica)(jnp.arange(REPLICAS, dtype=jnp.int32))


def draw_miss_ids(key, part):
    lists = plan_lists(key)
    return lists[0]


def draw_evict_slots(key, part):
    lists = plan_lists(key)
    return lists[1]


def draw_slot_ids(key, part):
    lists = plan_lists(key)
    return lists[2]


def draw_row_ids(key, part):
    lists = plan_lists(key)
    return lists[3].reshape(TOKENS)


def steps_of(rng, dims, cuts, least, largest):
    level = 1.0
    for axis_at, blocks in cuts:
        heights = jax.random.uniform(jax.random.fold_in(jax.random.fold_in(rng, 6), axis_at), (blocks,), jnp.float32, least / len(cuts), largest / len(cuts))
        level = level * jnp.repeat(jnp.exp(heights), dims[axis_at] // blocks).reshape((-1,) + (1,) * (len(dims) - 1 - axis_at))
    return level


def normal_values(stream_key, dims, spread, bound, shards=(), kind=jnp.bfloat16):
    drawn = spread * jax.random.normal(stream_key, dims, jnp.float32)
    if shards:
        drawn = drawn * steps_of(stream_key, dims, shards, -0.22, 0.18)
    return jnp.clip(drawn, -bound, bound).astype(kind)


def setup_inputs(seed: int = 0) -> dict:
    key_list = jax.random.split(jax.random.key(seed), 11)
    x_rows = normal_values(key_list[0], (TOKENS, D), 1.0, 6.0, ((0, 32), (1, 8)))
    v_weight = normal_values(key_list[1], (D, VW), D ** -0.5, 0.0625, ((1, 8),))
    home_a = normal_values(key_list[2], (ADAPTERS, R, D), D ** -0.5, 0.0625, ((0, 32), (2, 8)))
    home_b = normal_values(key_list[3], (ADAPTERS, R, VW), R ** -0.5, 0.75, ((0, 32), (2, 8)))
    cache_a = normal_values(key_list[4], (REPLICAS * CACHE, R, D), D ** -0.5, 0.0625, ((0, 32), (2, 8)))
    cache_b = normal_values(key_list[5], (REPLICAS * CACHE, R, VW), R ** -0.5, 0.75, ((0, 32), (2, 8)))
    miss_ids = draw_miss_ids(jax.random.fold_in(key_list[10], 71), 0)
    evict_slots = draw_evict_slots(jax.random.fold_in(key_list[10], 71), 0)
    slot_ids = draw_slot_ids(jax.random.fold_in(key_list[10], 71), 0)
    row_ids = draw_row_ids(jax.random.fold_in(key_list[10], 71), 0)
    return {"x_rows": x_rows, "v_weight": v_weight, "home_a": home_a, "home_b": home_b, "cache_a": cache_a, "cache_b": cache_b, "miss_ids": miss_ids, "evict_slots": evict_slots, "slot_ids": slot_ids, "row_ids": row_ids}


adapter_scale = 2.0


def reference(x_rows, v_weight, home_a, home_b, cache_a, cache_b, miss_ids, evict_slots, slot_ids, row_ids):
    def one_replica(replica):
        wanted = miss_ids[replica]
        evicted = evict_slots[replica]
        rows = lax.dynamic_slice_in_dim(x_rows, replica * ROWS, ROWS, 0)
        names = lax.dynamic_slice_in_dim(row_ids, replica * ROWS, ROWS, 0)
        held_a = lax.dynamic_slice_in_dim(cache_a, replica * CACHE, CACHE, 0).at[evicted].set(home_a[wanted])
        resident_up_factor = lax.dynamic_slice_in_dim(cache_b, replica * CACHE, CACHE, 0).at[evicted].set(home_b[wanted])
        table = slot_ids[replica].at[evicted].set(wanted)
        matches = names[:, None] == table[None, :]
        cache_entry_for = jnp.sum(jnp.where(matches, jnp.arange(CACHE, dtype=jnp.int32)[None, :], 0), axis=1).astype(jnp.int32)
        down = jnp.dot(rows, held_a.reshape(CACHE * R, D).T, preferred_element_type=jnp.float32).reshape(ROWS, CACHE, R)
        reduced_inner = jnp.take_along_axis(down, cache_entry_for[:, None, None], axis=1)[:, 0, :].astype(jnp.bfloat16)
        adapter_delta = jnp.einsum("uj,ujx->ux", reduced_inner.astype(jnp.float32), resident_up_factor[cache_entry_for].astype(jnp.float32))
        frozen_value = jnp.dot(rows, v_weight, preferred_element_type=jnp.float32)
        return (frozen_value + adapter_scale * adapter_delta).astype(jnp.bfloat16)

    result = lax.map(one_replica, jnp.arange(REPLICAS, dtype=jnp.int32))
    return result.reshape(TOKENS, VW)
```

```python
import functools

import jax
import jax.numpy as jnp
from jax import lax
from jax.experimental import pallas as pl
from jax.experimental.pallas import tpu as pltpu
from jax.sharding import PartitionSpec as P

adapter_scale = 2.0
room = 16
lanes = 128
bf16, f32, i32 = jnp.bfloat16, jnp.float32, jnp.int32


def call(kernel, out_shape, *args, smem=0, flops=0, limit=32 << 20):
    nbytes = sum(a.size * a.dtype.itemsize for a in args)
    nbytes += sum(o.size * o.dtype.itemsize for o in jax.tree.leaves(out_shape))
    specs = [pl.BlockSpec(memory_space=pltpu.SMEM)] * smem
    specs += [pl.BlockSpec(memory_space=pltpu.VMEM)] * (len(args) - smem)
    return pl.pallas_call(
        kernel,
        out_shape=out_shape,
        in_specs=specs,
        out_specs=jax.tree.map(lambda _: pl.BlockSpec(memory_space=pltpu.VMEM), out_shape),
        compiler_params=pltpu.CompilerParams(vmem_limit_bytes=limit),
        cost_estimate=pl.CostEstimate(flops=flops, bytes_accessed=nbytes, transcendentals=0),
    )(*args)


def column(row):
    n = row.shape[1]
    down = lax.broadcasted_iota(i32, (n, n), 0)
    across = lax.broadcasted_iota(i32, (n, n), 1)
    return jnp.sum(jnp.where(down == across, row, 0), axis=1, keepdims=True)


def targets(ids, me, turn, per_home):
    n = ids.shape[1]
    home = ids // per_home
    down = lax.broadcasted_iota(i32, (n, n), 0)
    across = lax.broadcasted_iota(i32, (n, n), 1)
    before = (column(home) == home) & (down < across)
    rank = jnp.sum(before.astype(i32), axis=0, keepdims=True)
    away = home != me
    most = jnp.max(jnp.where(away, rank + 1, 0))
    place = rank - turn * room
    sent = away & (place >= 0) & (place < room)
    return jnp.where(sent, home * room + place, -1), most


def spread(count, width, inner):
    at = lax.broadcasted_iota(i32, (width, count * inner), 0)
    col = lax.broadcasted_iota(i32, (width, count * inner), 1)
    return (col // inner == at).astype(bf16)


def dot(a, b):
    return jnp.dot(a, b, preferred_element_type=f32)


def dot_t(a, b):
    return lax.dot_general(a, b, (((1,), (1,)), ((), ())), preferred_element_type=f32)


def pack_kernel(per_home, where_ref, ids_ref, x_ref, out_ref):
    slots = out_ref.shape[0]
    width = x_ref.shape[1]
    ids = ids_ref[...]
    n = ids.shape[1]
    to, most = targets(ids, where_ref[0], where_ref[1], per_home)
    place = (lax.broadcasted_iota(i32, (slots, n), 0) == to).astype(bf16)
    out_ref[:, :width] = dot(place, x_ref[...]).astype(bf16)
    lane = lax.broadcasted_iota(i32, (n, lanes), 1)
    which = (lane == column(ids % per_home)).astype(bf16)
    tag = dot(place, which)
    lane = lax.broadcasted_iota(i32, (slots, lanes), 1)
    out_ref[:, width:] = jnp.where(lane == per_home, most.astype(f32), tag).astype(bf16)


def masked_down(x, pick, factors_ref, inner):
    step = 4 * inner
    total = None
    for at in range(0, factors_ref.shape[0], step):
        part = dot_t(x, factors_ref[at : at + step, :]) * pick(at, step)
        part = part[:, : 2 * inner] + part[:, 2 * inner :]
        total = part if total is None else total + part
    return total + pltpu.roll(total, inner, 1)


def fold(both, inner):
    half = both.shape[0] // 2
    lane = lax.broadcasted_iota(i32, (half, 2 * inner), 1)
    return jnp.where(lane < inner, both[:half], both[half:])


def unfold(folded, inner):
    half = folded.shape[0]
    lane = lax.broadcasted_iota(i32, (half, 2 * inner), 1)
    other = pltpu.roll(folded, inner, 1)
    return jnp.concatenate(
        [jnp.where(lane < inner, folded, other), jnp.where(lane < inner, other, folded)], axis=0
    )


def masked_up(both, pick, factors_ref, inner):
    step = 4 * inner
    wide = jnp.concatenate([both, both], axis=1)
    total = None
    for at in range(0, factors_ref.shape[0], step):
        part = dot((wide * pick(at, step)).astype(bf16), factors_ref[at : at + step, :])
        total = part if total is None else total + part
    return total


def picker(onehot, inner):
    width = onehot.shape[1]

    def pick(at, step):
        row = lax.broadcasted_iota(i32, (width, step), 0)
        col = lax.broadcasted_iota(i32, (width, step), 1)
        return dot(onehot, ((col + at) // inner == row).astype(bf16))

    return pick


def own_pick(ids_ref, slot_ref, evict_ref):
    ids = column(ids_ref[...])
    slot = slot_ref[...]
    count = slot.shape[1]
    at = lax.broadcasted_iota(i32, (lanes, lanes), 1)
    listed = column(evict_ref[...])
    gone = jnp.max((listed == lax.broadcasted_iota(i32, (listed.shape[0], count), 1)).astype(i32), axis=0, keepdims=True)
    hit = (ids == slot) & (gone == 0)
    hit = jnp.where(hit, 1.0, 0.0)
    del at
    return jnp.pad(hit, ((0, 0), (0, lanes - count))).astype(bf16)


def own_down_kernel(inner, ids_ref, slot_ref, evict_ref, x_ref, a_ref, out_ref):
    pick = picker(own_pick(ids_ref, slot_ref, evict_ref), inner)
    out_ref[...] = fold(masked_down(x_ref[...], pick, a_ref, inner), inner).astype(bf16)


def down_kernel(inner, got_ref, a_ref, out_ref):
    width = a_ref.shape[1]
    pick = picker(got_ref[:, width:], inner)
    out_ref[...] = fold(masked_down(got_ref[:, :width], pick, a_ref, inner), inner).astype(bf16)


def low_of(parts_ref, lo, hi, inner):
    total = parts_ref[0, lo:hi, :].astype(f32)
    for k in range(1, parts_ref.shape[0]):
        total = total + parts_ref[k, lo:hi, :].astype(f32)
    return unfold(total.astype(bf16).astype(f32), inner)


def up_kernel(inner, parts_ref, tag_ref, b_ref, out_ref):
    half = tag_ref.shape[0] // 2
    both = low_of(parts_ref, 0, half, inner)
    out_ref[...] = masked_up(both, picker(tag_ref[...], inner), b_ref, inner).astype(bf16)


def own_up_kernel(inner, at, ids_ref, slot_ref, evict_ref, parts_ref, b_ref, out_ref):
    pick = picker(own_pick(ids_ref, slot_ref, evict_ref), inner)
    both = low_of(parts_ref, at, parts_ref.shape[1], inner)
    out_ref[...] = masked_up(both, pick, b_ref, inner)


def add_kernel(per_home, where_ref, ids_ref, back_ref, total_ref, out_ref):
    slots = back_ref.shape[0]
    ids = ids_ref[...]
    n = ids.shape[1]
    to, _ = targets(ids, where_ref[0], where_ref[1], per_home)
    place = (lax.broadcasted_iota(i32, (slots, n), 0) == to).astype(bf16)
    came = lax.dot_general(place, back_ref[...], (((0,), (0,)), ((), ())), preferred_element_type=f32)
    out_ref[...] = total_ref[...] + adapter_scale * came


def swap(blocks, axis):
    return lax.all_to_all(blocks, axis, split_axis=0, concat_axis=0, tiled=True)


def shards(
    x_rows, v_weight, home_a, home_b, cache_a, cache_b, miss_ids, evict_slots, slot_ids, row_ids
):
    n, width = x_rows.shape
    per_home, inner, _ = home_a.shape
    cols = home_b.shape[2]
    replicas = lax.axis_size("replica")
    sides = lax.axis_size("tensor")
    slots = replicas * room
    me = lax.axis_index("replica").astype(i32)
    ids = row_ids.reshape(1, n)
    a_all = home_a.reshape(per_home * inner, width)
    b_all = home_b.reshape(per_home * inner, cols)
    kept_a = cache_a.reshape(-1, width)
    kept_b = cache_b.reshape(-1, cols)

    def send(turn):
        where = jnp.stack([me, turn.astype(i32)])
        packed = call(
            functools.partial(pack_kernel, per_home),
            jax.ShapeDtypeStruct((slots, width + lanes), bf16),
            where, ids, x_rows, smem=1, flops=2 * slots * n * width,
        )
        got = swap(packed.reshape(replicas, room, width + lanes), "replica")
        return where, got.reshape(slots, width + lanes)

    def down(got):
        return call(
            functools.partial(down_kernel, inner),
            jax.ShapeDtypeStruct((slots // 2, lanes), bf16),
            got, a_all, flops=2 * slots * width * per_home * inner,
        )

    def share(part):
        return swap(jnp.broadcast_to(part[None], (sides, *part.shape)), "tensor")

    def up(parts, got):
        back = call(
            functools.partial(up_kernel, inner),
            jax.ShapeDtypeStruct((slots, cols), bf16),
            parts, got[:, width:], b_all, flops=2 * slots * cols * per_home * inner,
        )
        return swap(back.reshape(replicas, room, cols), "replica").reshape(slots, cols)

    def add(where, back, total):
        return call(
            functools.partial(add_kernel, per_home),
            jax.ShapeDtypeStruct((n, cols), f32),
            where, ids, back, total, smem=1, flops=2 * slots * n * cols,
        )

    where, got = send(jnp.int32(0))
    whole = lax.all_gather(x_rows, "tensor", axis=1, tiled=True)
    own = call(
        functools.partial(own_down_kernel, inner),
        jax.ShapeDtypeStruct((n // 2, lanes), bf16),
        ids, slot_ids, evict_slots, x_rows, kept_a, flops=2 * n * width * kept_a.shape[0],
    )
    most = jnp.max(got[:, width + per_home].astype(f32)).astype(i32)
    turns = (most + room - 1) // room
    parts = share(jnp.concatenate([down(got), own], axis=0))
    base = jnp.dot(whole, v_weight, preferred_element_type=f32)
    own_lora = call(
        functools.partial(own_up_kernel, inner, slots // 2),
        jax.ShapeDtypeStruct((n, cols), f32),
        ids, slot_ids, evict_slots, parts, kept_b, flops=2 * n * cols * kept_b.shape[0],
    )
    total = add(where, up(parts, got), base + adapter_scale * own_lora)

    def again(state):
        turn, total = state
        where, got = send(turn)
        return turn + 1, add(where, up(share(down(got)), got), total)

    _, total = lax.while_loop(lambda s: s[0] < turns, again, (jnp.int32(1), total))
    return total.astype(bf16)


def solution(mesh):
    return jax.shard_map(
        shards,
        mesh=mesh,
        in_specs=(
            P("replica", "tensor"),
            P(None, "tensor"),
            P("replica", None, "tensor"),
            P("replica", None, "tensor"),
            P("replica", None, "tensor"),
            P("replica", None, "tensor"),
            P("replica", None),
            P("replica", None),
            P("replica", None),
            P("replica"),
        ),
        out_specs=P("replica", "tensor"),
        check_vma=False,
    )
```

```python
import functools

import jax
import jax.numpy as jnp
from jax import lax
from jax.experimental import pallas as pl
from jax.experimental.pallas import tpu as pltpu
from jax.sharding import PartitionSpec as P

adapter_scale = 2.0
room = 16
fits = 160
first_count = 64
lanes = 128
bf16, f32, i32 = jnp.bfloat16, jnp.float32, jnp.int32


def call(kernel, out_shape, *args, smem=0, smem_out=0, us=1, limit=8 << 20):
    scalar, whole = pl.BlockSpec(memory_space=pltpu.SMEM), pl.BlockSpec(memory_space=pltpu.VMEM)
    several = isinstance(out_shape, tuple)
    results = len(out_shape) if several else 1
    out_specs = (whole,) * (results - smem_out) + (scalar,) * smem_out
    return pl.pallas_call(
        kernel,
        out_shape=out_shape,
        in_specs=[scalar] * smem + [whole] * (len(args) - smem),
        out_specs=out_specs if several else out_specs[0],
        compiler_params=pltpu.CompilerParams(vmem_limit_bytes=limit),
        cost_estimate=pl.CostEstimate(flops=0, bytes_accessed=us * 3_000_000, transcendentals=0),
    )(*args)


def column(row):
    n = row.shape[1]
    down = lax.broadcasted_iota(i32, (n, n), 0)
    across = lax.broadcasted_iota(i32, (n, n), 1)
    return jnp.sum(jnp.where(down == across, row, 0), axis=1, keepdims=True)


def ranks(home, todo):
    n = home.shape[1]
    down = lax.broadcasted_iota(i32, (n, n), 0)
    across = lax.broadcasted_iota(i32, (n, n), 1)
    before = (column(home) == home) & (column(todo) > 0) & (down < across)
    return jnp.sum(before.astype(i32), axis=0, keepdims=True)


def targets(home, todo):
    rank = ranks(home, todo)
    return jnp.where((todo > 0) & (rank < room), home * room + rank, -1)


def dot(a, b):
    return jnp.dot(a, b, preferred_element_type=f32)


def dot_t(a, b):
    return lax.dot_general(a, b, (((1,), (1,)), ((), ())), preferred_element_type=f32)


def pack_kernel(per_home, me_ref, ids_ref, todo_ref, x_ref, out_ref):
    slots = out_ref.shape[0]
    width = x_ref.shape[1]
    ids = ids_ref[...]
    n = ids.shape[1]
    home = ids // per_home
    todo = jnp.where(home != me_ref[0], todo_ref[...], 0)
    to = targets(home, todo)
    place = (lax.broadcasted_iota(i32, (slots, n), 0) == to).astype(bf16)
    out_ref[:, :width] = dot(place, x_ref[...]).astype(bf16)
    lane = lax.broadcasted_iota(i32, (n, lanes), 1)
    which = (lane == column(ids % per_home)).astype(bf16)
    tag = dot(place, which)
    wanted = (lane == column(home) + first_count) & (column(todo) > 0)
    counts = jnp.sum(wanted.astype(f32), axis=0, keepdims=True)
    lane = lax.broadcasted_iota(i32, (slots, lanes), 1)
    out_ref[:, width:] = jnp.where(lane >= first_count, counts, tag).astype(bf16)


def left_kernel(per_home, fits, me_ref, ids_ref, count_ref, todo_ref, turns_ref):
    ids = ids_ref[...]
    home = ids // per_home
    away = home != me_ref[0]
    todo = away.astype(i32)
    counts = count_ref[...]
    replicas = counts.shape[0]
    sent = jnp.minimum(counts, float(room))
    down = lax.broadcasted_iota(i32, (replicas, replicas), 0)
    across = lax.broadcasted_iota(i32, (replicas, replicas), 1)
    ahead = dot((across < down).astype(bf16), sent.astype(bf16))
    left = counts - jnp.clip(float(fits) - ahead, 0.0, sent)
    lane = lax.broadcasted_iota(i32, (replicas, lanes), 1)
    most = jnp.max(jnp.where(lane >= first_count, left, 0.0)).astype(i32)
    turns_ref[0] = (most + room - 1) // room
    mine = lax.broadcasted_iota(i32, (replicas, lanes), 0) == me_ref[0]
    mine = jnp.sum(jnp.where(mine, ahead, 0.0), axis=0, keepdims=True).astype(i32)
    at = lax.broadcasted_iota(i32, (lanes, home.shape[1]), 0)
    mine = jnp.sum(jnp.where(at == home + first_count, column(mine), 0), axis=0, keepdims=True)
    rank = ranks(home, todo)
    served = (rank < room) & (mine + rank < fits)
    todo_ref[...] = jnp.where(away & ~served, 1, 0)


def masked_down(x, pick, factors_ref, inner):
    step = 4 * inner
    total = None
    for at in range(0, factors_ref.shape[0], step):
        part = dot_t(x, factors_ref[at : at + step, :]) * pick(at, step)
        part = part[:, : 2 * inner] + part[:, 2 * inner :]
        total = part if total is None else total + part
    return total + pltpu.roll(total, inner, 1)


def fold(both, inner):
    half = both.shape[0] // 2
    lane = lax.broadcasted_iota(i32, (half, 2 * inner), 1)
    return jnp.where(lane < inner, both[:half], both[half:])


def unfold(folded, inner):
    half = folded.shape[0]
    lane = lax.broadcasted_iota(i32, (half, 2 * inner), 1)
    other = pltpu.roll(folded, inner, 1)
    return jnp.concatenate(
        [jnp.where(lane < inner, folded, other), jnp.where(lane < inner, other, folded)], axis=0
    )


def masked_up(both, pick, factors_ref, inner):
    step = 4 * inner
    wide = jnp.concatenate([both, both], axis=1)
    total = None
    for at in range(0, factors_ref.shape[0], step):
        part = dot((wide * pick(at, step)).astype(bf16), factors_ref[at : at + step, :])
        total = part if total is None else total + part
    return total


def picker(onehot, inner):
    width = onehot.shape[1]

    def pick(at, step):
        row = lax.broadcasted_iota(i32, (width, step), 0)
        col = lax.broadcasted_iota(i32, (width, step), 1)
        return dot(onehot, ((col + at) // inner == row).astype(bf16))

    return pick


def own_pick(ids_ref, slot_ref, evict_ref):
    ids = column(ids_ref[...])
    slot = slot_ref[...]
    count = slot.shape[1]
    listed = column(evict_ref[...])
    gone = jnp.max((listed == lax.broadcasted_iota(i32, (listed.shape[0], count), 1)).astype(i32), axis=0, keepdims=True)
    hit = (ids == slot) & (gone == 0)
    hit = jnp.where(hit, 1.0, 0.0)
    return jnp.pad(hit, ((0, 0), (0, lanes - count))).astype(bf16)


def own_down_kernel(inner, ids_ref, slot_ref, evict_ref, x_ref, a_ref, out_ref):
    pick = picker(own_pick(ids_ref, slot_ref, evict_ref), inner)
    out_ref[...] = fold(masked_down(x_ref[...], pick, a_ref, inner), inner).astype(bf16)


def kept_slots(at_ref, held):
    at = at_ref[...]
    return (lax.broadcasted_iota(i32, (held, at.shape[1]), 0) == at).astype(bf16)


def down_kernel(inner, per_home, got_ref, a_ref, *refs):
    own_ref = refs[0] if len(refs) == 5 else None
    out_ref, name_ref, at_ref, count_ref = refs[-4:]
    slots = got_ref.shape[0]
    width = a_ref.shape[1]
    held = name_ref.shape[0]
    tag = got_ref[:, width:]
    lane = lax.broadcasted_iota(i32, (16, lanes), 1)
    full = dot_t((lane < per_home).astype(bf16), tag)
    down = lax.broadcasted_iota(i32, (slots, slots), 0)
    across = lax.broadcasted_iota(i32, (slots, slots), 1)
    at = dot(full.astype(bf16), (down < across).astype(bf16))
    at_ref[...] = jnp.where(full > 0.5, at, -1.0)[:1].astype(i32)
    keep = kept_slots(at_ref, held)
    x = dot(keep, got_ref[:, :width]).astype(bf16)
    name = dot(keep, tag)
    lane = lax.broadcasted_iota(i32, (held, lanes), 1)
    name = jnp.where(lane < per_home, name, 0.0).astype(bf16)
    name_ref[...] = name
    part = fold(masked_down(x, picker(name, inner), a_ref, inner), inner).astype(bf16)
    for side in range(out_ref.shape[0]):
        out_ref[side, : held // 2, :] = part
        if own_ref is not None:
            out_ref[side, held // 2 :, :] = own_ref[...]
    for r in range(count_ref.shape[0]):
        count_ref[r : r + 1, :] = got_ref[r * room : r * room + 1, width:].astype(f32)


def low_of(parts_ref, lo, hi, inner):
    total = parts_ref[0, lo:hi, :].astype(f32)
    for k in range(1, parts_ref.shape[0]):
        total = total + parts_ref[k, lo:hi, :].astype(f32)
    return unfold(total.astype(bf16).astype(f32), inner)


def up_kernel(inner, parts_ref, name_ref, at_ref, b_ref, out_ref):
    keep = kept_slots(at_ref, name_ref.shape[0])
    half = name_ref.shape[0] // 2
    both = low_of(parts_ref, 0, half, inner)
    lora = masked_up(both, picker(name_ref[...], inner), b_ref, inner).astype(bf16)
    back = lax.dot_general(keep, lora, (((0,), (0,)), ((), ())), preferred_element_type=f32)
    out_ref[...] = back.astype(bf16)


def own_up_kernel(inner, at, ids_ref, slot_ref, evict_ref, parts_ref, b_ref, out_ref):
    pick = picker(own_pick(ids_ref, slot_ref, evict_ref), inner)
    both = low_of(parts_ref, at, parts_ref.shape[1], inner)
    out_ref[...] = masked_up(both, pick, b_ref, inner)


def base_kernel(steps, side_ref, w_ref, *refs):
    *total, out_ref = refs
    blocks = total[-len(steps) :]
    sum_ = total[0][...] if len(total) > len(steps) else None
    width = blocks[0].shape[1]
    sides = w_ref.shape[0] // width
    for block, step in zip(blocks, steps, strict=True):
        side = lax.rem(side_ref[0] + step, sides)
        weight = w_ref[pl.ds(pl.multiple_of(side * width, width), width), :]
        part = dot(block[...], weight)
        sum_ = part if sum_ is None else sum_ + part
    out_ref[...] = sum_


def came_back(per_home, me_ref, ids_ref, todo_ref, back_ref):
    slots = back_ref.shape[0]
    home = ids_ref[...] // per_home
    todo = jnp.where(home != me_ref[0], todo_ref[...], 0)
    place = (lax.broadcasted_iota(i32, (slots, home.shape[1]), 0) == targets(home, todo)).astype(bf16)
    return lax.dot_general(place, back_ref[...], (((0,), (0,)), ((), ())), preferred_element_type=f32)


def last_kernel(per_home, me_ref, ids_ref, todo_ref, back_ref, base_ref, own_ref, more_ref, out_ref):
    came = came_back(per_home, me_ref, ids_ref, todo_ref, back_ref)
    lora = own_ref[...] + more_ref[...] + came
    out_ref[...] = (base_ref[...] + adapter_scale * lora).astype(bf16)


def more_kernel(per_home, me_ref, ids_ref, todo_ref, back_ref, more_ref, out_ref, left_ref):
    out_ref[...] = more_ref[...] + came_back(per_home, me_ref, ids_ref, todo_ref, back_ref)
    home = ids_ref[...] // per_home
    todo = todo_ref[...]
    left_ref[...] = jnp.where(ranks(home, todo) < room, 0, todo)


def swap(blocks, axis):
    return lax.all_to_all(blocks, axis, split_axis=0, concat_axis=0, tiled=True)


def shards(
    x_rows, v_weight, home_a, home_b, cache_a, cache_b, miss_ids, evict_slots, slot_ids, row_ids
):
    n, width = x_rows.shape
    per_home, inner, _ = home_a.shape
    cols = home_b.shape[2]
    replicas = lax.axis_size("replica")
    sides = lax.axis_size("tensor")
    slots = replicas * room
    me = lax.axis_index("replica").astype(i32).reshape(1)
    side = lax.axis_index("tensor").astype(i32).reshape(1)
    ids = row_ids.reshape(1, n)
    a_all = home_a.reshape(per_home * inner, width)
    b_all = home_b.reshape(per_home * inner, cols)

    def send(todo):
        packed = call(
            functools.partial(pack_kernel, per_home),
            jax.ShapeDtypeStruct((slots, width + lanes), bf16),
            me, ids, todo, x_rows, smem=1, us=3,
        )
        got = swap(packed.reshape(replicas, room, width + lanes), "replica")
        return got.reshape(slots, width + lanes)

    def down(got, held, *own):
        rows = held // 2 + sum(o.shape[0] for o in own)
        out = (
            jax.ShapeDtypeStruct((sides, rows, lanes), bf16),
            jax.ShapeDtypeStruct((held, lanes), bf16),
            jax.ShapeDtypeStruct((1, slots), i32),
            jax.ShapeDtypeStruct((replicas, lanes), f32),
        )
        return call(functools.partial(down_kernel, inner, per_home), out, got, a_all, *own, us=3)

    def up(parts, name, at):
        return call(
            functools.partial(up_kernel, inner),
            jax.ShapeDtypeStruct((slots, cols), bf16),
            parts, name, at, b_all, us=2,
        )

    def give(back):
        return swap(back.reshape(replicas, room, cols), "replica").reshape(slots, cols)

    todo = jnp.ones((1, n), i32)
    got = send(todo)
    own = call(
        functools.partial(own_down_kernel, inner),
        jax.ShapeDtypeStruct((n // 2, lanes), bf16),
        ids, slot_ids, evict_slots, x_rows, cache_a.reshape(-1, width), us=3, limit=16 << 20,
    )

    def shift(block, by):
        return lax.ppermute(block, "tensor", [(k, (k + by) % sides) for k in range(sides)])

    def base(total, home_step, blocks):
        steps = tuple(s % sides for s in home_step)
        return call(
            functools.partial(base_kernel, steps), jax.ShapeDtypeStruct((n, cols), f32),
            side, v_weight, *total, *blocks, smem=1,
        )

    near = [shift(x_rows, step) for step in (1, -1, 2, -2)]
    part, name, at, counts = down(got, fits, own)
    part, *near = lax.optimization_barrier((part, *near))
    parts = swap(part, "tensor")
    far = [shift(near[2], 1), shift(near[3], -1), shift(near[2], 2)]
    frozen = base((), (0, -1, 1, -2, 2), (x_rows, *near))
    unserved, turns = call(
        functools.partial(left_kernel, per_home, fits),
        (jax.ShapeDtypeStruct((1, n), i32), jax.ShapeDtypeStruct((1,), i32)),
        me, ids, counts, smem=1, smem_out=1, us=2,
    )
    parts, frozen, unserved, turns = lax.optimization_barrier((parts, frozen, unserved, turns))
    back = give(up(parts, name, at))
    own_lora = call(
        functools.partial(own_up_kernel, inner, fits // 2),
        jax.ShapeDtypeStruct((n, cols), f32),
        ids, slot_ids, evict_slots, parts, cache_b.reshape(-1, cols),
    )
    frozen = base((frozen,), (-3, 3, 4), far)
    unserved, turns, back = lax.optimization_barrier((unserved, turns, back))

    def again(state):
        turn, unserved, more = state
        part, name, at, _ = down(send(unserved), slots)
        back = give(up(swap(part, "tensor"), name, at))
        more, unserved = call(
            functools.partial(more_kernel, per_home),
            (jax.ShapeDtypeStruct((n, cols), f32), jax.ShapeDtypeStruct((1, n), i32)),
            me, ids, unserved, back, more, smem=1,
        )
        return turn + 1, unserved, more

    state = (jnp.int32(0), unserved, jnp.zeros((n, cols), f32))
    _, _, more = lax.while_loop(lambda s: s[0] < turns[0], again, state)
    return call(
        functools.partial(last_kernel, per_home),
        jax.ShapeDtypeStruct((n, cols), bf16),
        me, ids, todo, back, frozen, own_lora, more, smem=1,
    )


def solution(mesh):
    return jax.shard_map(
        shards,
        mesh=mesh,
        in_specs=(
            P("replica", "tensor"),
            P(None, "tensor"),
            P("replica", None, "tensor"),
            P("replica", None, "tensor"),
            P("replica", None, "tensor"),
            P("replica", None, "tensor"),
            P("replica", None),
            P("replica", None),
            P("replica", None),
            P("replica"),
        ),
        out_specs=P("replica", "tensor"),
        check_vma=False,
    )
```

```python
import functools

import jax
import jax.numpy as jnp
from jax import lax
from jax.experimental import pallas as pl
from jax.experimental.pallas import tpu as pltpu
from jax.sharding import PartitionSpec as P

adapter_scale = 2.0
room = 16
fits = 160
first_count = 64
lanes = 128
bf16, f32, i32 = jnp.bfloat16, jnp.float32, jnp.int32


def call(kernel, out_shape, *args, smem=0, smem_out=0, us=1, limit=8 << 20):
    scalar, whole = pl.BlockSpec(memory_space=pltpu.SMEM), pl.BlockSpec(memory_space=pltpu.VMEM)
    several = isinstance(out_shape, tuple)
    results = len(out_shape) if several else 1
    out_specs = (whole,) * (results - smem_out) + (scalar,) * smem_out
    return pl.pallas_call(
        kernel,
        out_shape=out_shape,
        in_specs=[scalar] * smem + [whole] * (len(args) - smem),
        out_specs=out_specs if several else out_specs[0],
        compiler_params=pltpu.CompilerParams(vmem_limit_bytes=limit),
        cost_estimate=pl.CostEstimate(flops=0, bytes_accessed=us * 3_000_000, transcendentals=0),
    )(*args)


def column(row):
    n = row.shape[1]
    down = lax.broadcasted_iota(i32, (n, n), 0)
    across = lax.broadcasted_iota(i32, (n, n), 1)
    return jnp.sum(jnp.where(down == across, row, 0), axis=1, keepdims=True)


def ranks(home, home_at, sent_at):
    n = home.shape[1]
    down = lax.broadcasted_iota(i32, (n, n), 0)
    across = lax.broadcasted_iota(i32, (n, n), 1)
    before = (home_at == home) & sent_at & (down < across)
    return jnp.sum(before.astype(i32), axis=0, keepdims=True)


def dot(a, b):
    return jnp.dot(a, b, preferred_element_type=f32)


def dot_t(a, b):
    return lax.dot_general(a, b, (((1,), (1,)), ((), ())), preferred_element_type=f32)


def pack_kernel(per_home, me_ref, ids_ref, *refs):
    *todo, x_ref, out_ref, to_ref = refs
    slots = out_ref.shape[0]
    width = x_ref.shape[1]
    ids = ids_ref[...]
    n = ids.shape[1]
    ids_at = column(ids)
    home, home_at = ids // per_home, ids_at // per_home
    sent, sent_at = home != me_ref[0], home_at != me_ref[0]
    if todo:
        sent = sent & (todo[0][...] > 0)
        sent_at = sent_at & (column(todo[0][...]) > 0)
    rank = ranks(home, home_at, sent_at)
    to = jnp.where(sent & (rank < room), home * room + rank, -1)
    to_ref[...] = to
    place = (lax.broadcasted_iota(i32, (slots, n), 0) == to).astype(bf16)
    out_ref[:, :width] = dot(place, x_ref[...]).astype(bf16)
    lane = lax.broadcasted_iota(i32, (n, lanes), 1)
    which = (lane == ids_at % per_home).astype(bf16)
    tag = dot(place, which)
    wanted = (lane == home_at + first_count) & sent_at
    counts = jnp.sum(wanted.astype(f32), axis=0, keepdims=True)
    lane = lax.broadcasted_iota(i32, (slots, lanes), 1)
    out_ref[:, width:] = jnp.where(lane >= first_count, counts, tag).astype(bf16)


def left_kernel(per_home, fits, me_ref, ids_ref, count_ref, todo_ref, turns_ref):
    ids = ids_ref[...]
    home = ids // per_home
    away = home != me_ref[0]
    counts = count_ref[...]
    replicas = counts.shape[0]
    sent = jnp.minimum(counts, float(room))
    down = lax.broadcasted_iota(i32, (replicas, replicas), 0)
    across = lax.broadcasted_iota(i32, (replicas, replicas), 1)
    ahead = dot((across < down).astype(bf16), sent.astype(bf16))
    left = counts - jnp.clip(float(fits) - ahead, 0.0, sent)
    lane = lax.broadcasted_iota(i32, (replicas, lanes), 1)
    most = jnp.max(jnp.where(lane >= first_count, left, 0.0)).astype(i32)
    turns_ref[0] = (most + room - 1) // room
    mine = lax.broadcasted_iota(i32, (replicas, lanes), 0) == me_ref[0]
    mine = jnp.sum(jnp.where(mine, ahead, 0.0), axis=0, keepdims=True).astype(i32)
    at = lax.broadcasted_iota(i32, (lanes, home.shape[1]), 0)
    mine = jnp.sum(jnp.where(at == home + first_count, column(mine), 0), axis=0, keepdims=True)
    home_at = column(home)
    rank = ranks(home, home_at, home_at != me_ref[0])
    served = (rank < room) & (mine + rank < fits)
    todo_ref[...] = jnp.where(away & ~served, 1, 0)


def masked_down(x, pick, factors_ref, inner):
    step = 4 * inner
    total = None
    for at in range(0, factors_ref.shape[0], step):
        part = dot_t(x, factors_ref[at : at + step, :]) * pick(at, step)
        part = part[:, : 2 * inner] + part[:, 2 * inner :]
        total = part if total is None else total + part
    return total + pltpu.roll(total, inner, 1)


def fold(both, inner):
    half = both.shape[0] // 2
    lane = lax.broadcasted_iota(i32, (half, 2 * inner), 1)
    return jnp.where(lane < inner, both[:half], both[half:])


def unfold(folded, inner):
    half = folded.shape[0]
    lane = lax.broadcasted_iota(i32, (half, 2 * inner), 1)
    other = pltpu.roll(folded, inner, 1)
    return jnp.concatenate(
        [jnp.where(lane < inner, folded, other), jnp.where(lane < inner, other, folded)], axis=0
    )


def masked_up(both, pick, factors_ref, inner):
    step = 4 * inner
    wide = jnp.concatenate([both, both], axis=1)
    total = None
    for at in range(0, factors_ref.shape[0], step):
        part = dot((wide * pick(at, step)).astype(bf16), factors_ref[at : at + step, :])
        total = part if total is None else total + part
    return total


def picker(onehot, inner):
    width = onehot.shape[1]

    def pick(at, step):
        row = lax.broadcasted_iota(i32, (width, step), 0)
        col = lax.broadcasted_iota(i32, (width, step), 1)
        return dot(onehot, ((col + at) // inner == row).astype(bf16))

    return pick


def own_pick(ids_ref, slot_ref, evict_ref):
    ids = column(ids_ref[...])
    slot = slot_ref[...]
    count = slot.shape[1]
    listed = column(evict_ref[...])
    gone = jnp.max((listed == lax.broadcasted_iota(i32, (listed.shape[0], count), 1)).astype(i32), axis=0, keepdims=True)
    hit = (ids == slot) & (gone == 0)
    hit = jnp.where(hit, 1.0, 0.0)
    return jnp.pad(hit, ((0, 0), (0, lanes - count))).astype(bf16)


def own_down_kernel(inner, ids_ref, slot_ref, evict_ref, x_ref, a_ref, out_ref):
    pick = picker(own_pick(ids_ref, slot_ref, evict_ref), inner)
    out_ref[...] = fold(masked_down(x_ref[...], pick, a_ref, inner), inner).astype(bf16)


def kept_slots(at_ref, held):
    at = at_ref[...]
    return (lax.broadcasted_iota(i32, (held, at.shape[1]), 0) == at).astype(bf16)


def down_kernel(inner, per_home, got_ref, a_ref, *refs):
    own_ref = refs[0] if len(refs) == 5 else None
    out_ref, name_ref, at_ref, count_ref = refs[-4:]
    slots = got_ref.shape[0]
    width = a_ref.shape[1]
    held = name_ref.shape[0]
    tag = got_ref[:, width:]
    lane = lax.broadcasted_iota(i32, (16, lanes), 1)
    full = dot_t((lane < per_home).astype(bf16), tag)
    down = lax.broadcasted_iota(i32, (slots, slots), 0)
    across = lax.broadcasted_iota(i32, (slots, slots), 1)
    at = dot(full.astype(bf16), (down < across).astype(bf16))
    at_ref[...] = jnp.where(full > 0.5, at, -1.0)[:1].astype(i32)
    keep = kept_slots(at_ref, held)
    x = dot(keep, got_ref[:, :width]).astype(bf16)
    name = dot(keep, tag)
    lane = lax.broadcasted_iota(i32, (held, lanes), 1)
    name = jnp.where(lane < per_home, name, 0.0).astype(bf16)
    name_ref[...] = name
    part = fold(masked_down(x, picker(name, inner), a_ref, inner), inner).astype(bf16)
    for side in range(out_ref.shape[0]):
        out_ref[side, : held // 2, :] = part
        if own_ref is not None:
            out_ref[side, held // 2 :, :] = own_ref[...]
    for r in range(count_ref.shape[0]):
        count_ref[r : r + 1, :] = got_ref[r * room : r * room + 1, width:].astype(f32)


def low_of(parts_ref, lo, hi, inner):
    total = parts_ref[0, lo:hi, :].astype(f32)
    for k in range(1, parts_ref.shape[0]):
        total = total + parts_ref[k, lo:hi, :].astype(f32)
    return unfold(total.astype(bf16).astype(f32), inner)


def up_kernel(inner, parts_ref, name_ref, at_ref, b_ref, out_ref):
    keep = kept_slots(at_ref, name_ref.shape[0])
    half = name_ref.shape[0] // 2
    both = low_of(parts_ref, 0, half, inner)
    lora = masked_up(both, picker(name_ref[...], inner), b_ref, inner).astype(bf16)
    back = lax.dot_general(keep, lora, (((0,), (0,)), ((), ())), preferred_element_type=f32)
    out_ref[...] = back.astype(bf16)


def own_up_kernel(inner, at, ids_ref, slot_ref, evict_ref, parts_ref, b_ref, out_ref):
    pick = picker(own_pick(ids_ref, slot_ref, evict_ref), inner)
    both = low_of(parts_ref, at, parts_ref.shape[1], inner)
    out_ref[...] = masked_up(both, pick, b_ref, inner)


def base_kernel(steps, side_ref, w_ref, *refs):
    *total, out_ref = refs
    blocks = total[-len(steps) :]
    sum_ = total[0][...] if len(total) > len(steps) else None
    width = blocks[0].shape[1]
    sides = w_ref.shape[0] // width
    for block, step in zip(blocks, steps, strict=True):
        side = lax.rem(side_ref[0] + step, sides)
        weight = w_ref[pl.ds(pl.multiple_of(side * width, width), width), :]
        part = dot(block[...], weight)
        sum_ = part if sum_ is None else sum_ + part
    out_ref[...] = sum_


def came_back(to_ref, back_ref):
    slots = back_ref.shape[0]
    place = (lax.broadcasted_iota(i32, (slots, to_ref.shape[1]), 0) == to_ref[...]).astype(bf16)
    return lax.dot_general(place, back_ref[...], (((0,), (0,)), ((), ())), preferred_element_type=f32)


def last_kernel(to_ref, back_ref, base_ref, own_ref, more_ref, out_ref):
    lora = own_ref[...] + more_ref[...] + came_back(to_ref, back_ref)
    out_ref[...] = (base_ref[...] + adapter_scale * lora).astype(bf16)


def more_kernel(to_ref, todo_ref, back_ref, more_ref, out_ref, left_ref):
    out_ref[...] = more_ref[...] + came_back(to_ref, back_ref)
    left_ref[...] = jnp.where(to_ref[...] >= 0, 0, todo_ref[...])


def swap(blocks, axis):
    return lax.all_to_all(blocks, axis, split_axis=0, concat_axis=0, tiled=True)


def shards(
    x_rows, v_weight, home_a, home_b, cache_a, cache_b, miss_ids, evict_slots, slot_ids, row_ids
):
    n, width = x_rows.shape
    per_home, inner, _ = home_a.shape
    cols = home_b.shape[2]
    replicas = lax.axis_size("replica")
    sides = lax.axis_size("tensor")
    slots = replicas * room
    me = lax.axis_index("replica").astype(i32).reshape(1)
    side = lax.axis_index("tensor").astype(i32).reshape(1)
    ids = row_ids.reshape(1, n)
    a_all = home_a.reshape(per_home * inner, width)
    b_all = home_b.reshape(per_home * inner, cols)

    def send(*todo):
        packed, to = call(
            functools.partial(pack_kernel, per_home),
            (jax.ShapeDtypeStruct((slots, width + lanes), bf16), jax.ShapeDtypeStruct((1, n), i32)),
            me, ids, *todo, x_rows, smem=1, us=3,
        )
        got = swap(packed.reshape(replicas, room, width + lanes), "replica")
        return got.reshape(slots, width + lanes), to

    def down(got, held, *own):
        rows = held // 2 + sum(o.shape[0] for o in own)
        out = (
            jax.ShapeDtypeStruct((sides, rows, lanes), bf16),
            jax.ShapeDtypeStruct((held, lanes), bf16),
            jax.ShapeDtypeStruct((1, slots), i32),
            jax.ShapeDtypeStruct((replicas, lanes), f32),
        )
        return call(functools.partial(down_kernel, inner, per_home), out, got, a_all, *own, us=3)

    def up(parts, name, at):
        return call(
            functools.partial(up_kernel, inner),
            jax.ShapeDtypeStruct((slots, cols), bf16),
            parts, name, at, b_all, us=2,
        )

    def give(back):
        return swap(back.reshape(replicas, room, cols), "replica").reshape(slots, cols)

    got, to = send()
    own = call(
        functools.partial(own_down_kernel, inner),
        jax.ShapeDtypeStruct((n // 2, lanes), bf16),
        ids, slot_ids, evict_slots, x_rows, cache_a.reshape(-1, width), us=3, limit=16 << 20,
    )

    def shift(block, by):
        return lax.ppermute(block, "tensor", [(k, (k + by) % sides) for k in range(sides)])

    def base(total, home_step, blocks):
        steps = tuple(s % sides for s in home_step)
        return call(
            functools.partial(base_kernel, steps), jax.ShapeDtypeStruct((n, cols), f32),
            side, v_weight, *total, *blocks, smem=1,
        )

    near = [shift(x_rows, step) for step in (1, -1, 2, -2)]
    part, name, at, counts = down(got, fits, own)
    part, *near = lax.optimization_barrier((part, *near))
    parts = swap(part, "tensor")
    far = [shift(near[2], 1), shift(near[3], -1), shift(near[2], 2)]
    frozen = base((), (0, -1, 1, -2, 2), (x_rows, *near))
    unserved, turns = call(
        functools.partial(left_kernel, per_home, fits),
        (jax.ShapeDtypeStruct((1, n), i32), jax.ShapeDtypeStruct((1,), i32)),
        me, ids, counts, smem=1, smem_out=1, us=2,
    )
    parts, frozen, unserved, turns = lax.optimization_barrier((parts, frozen, unserved, turns))
    back = give(up(parts, name, at))
    own_lora = call(
        functools.partial(own_up_kernel, inner, fits // 2),
        jax.ShapeDtypeStruct((n, cols), f32),
        ids, slot_ids, evict_slots, parts, cache_b.reshape(-1, cols),
    )
    frozen = base((frozen,), (-3, 3, 4), far)
    unserved, turns, back = lax.optimization_barrier((unserved, turns, back))

    def again(state):
        turn, unserved, more = state
        got, to = send(unserved)
        part, name, at, _ = down(got, slots)
        back = give(up(swap(part, "tensor"), name, at))
        more, unserved = call(
            more_kernel,
            (jax.ShapeDtypeStruct((n, cols), f32), jax.ShapeDtypeStruct((1, n), i32)),
            to, unserved, back, more,
        )
        return turn + 1, unserved, more

    state = (jnp.int32(0), unserved, jnp.zeros((n, cols), f32))
    _, _, more = lax.while_loop(lambda s: s[0] < turns[0], again, state)
    return call(
        last_kernel,
        jax.ShapeDtypeStruct((n, cols), bf16),
        to, back, frozen, own_lora, more,
    )


def solution(mesh):
    return jax.shard_map(
        shards,
        mesh=mesh,
        in_specs=(
            P("replica", "tensor"),
            P(None, "tensor"),
            P("replica", None, "tensor"),
            P("replica", None, "tensor"),
            P("replica", None, "tensor"),
            P("replica", None, "tensor"),
            P("replica", None),
            P("replica", None),
            P("replica", None),
            P("replica"),
        ),
        out_specs=P("replica", "tensor"),
        check_vma=False,
    )
```

```python
import functools

import jax
import jax.numpy as jnp
from jax import lax
from jax.experimental import pallas as pl
from jax.experimental.pallas import tpu as pltpu
from jax.sharding import PartitionSpec as P

adapter_scale = 2.0
room = 16
fits = 160
first_count = 64
lanes = 128
bf16, f32, i32 = jnp.bfloat16, jnp.float32, jnp.int32


def call(kernel, out_shape, *args, smem=0, smem_out=0, hbm_out=0, scratch=(), us=1, limit=8 << 20):
    scalar, whole = pl.BlockSpec(memory_space=pltpu.SMEM), pl.BlockSpec(memory_space=pltpu.VMEM)
    several = isinstance(out_shape, tuple)
    results = len(out_shape) if several else 1
    out_specs = (pl.BlockSpec(memory_space=pltpu.HBM),) * hbm_out
    out_specs += (whole,) * (results - smem_out - hbm_out) + (scalar,) * smem_out
    return pl.pallas_call(
        kernel,
        out_shape=out_shape,
        in_specs=[scalar] * smem + [whole] * (len(args) - smem),
        out_specs=out_specs if several else out_specs[0],
        scratch_shapes=scratch,
        compiler_params=pltpu.CompilerParams(vmem_limit_bytes=limit),
        cost_estimate=pl.CostEstimate(flops=0, bytes_accessed=us * 3_000_000, transcendentals=0),
    )(*args)


def column(row):
    n = row.shape[1]
    down = lax.broadcasted_iota(i32, (n, n), 0)
    across = lax.broadcasted_iota(i32, (n, n), 1)
    return jnp.sum(jnp.where(down == across, row, 0), axis=1, keepdims=True)


def ranks(home, home_at, sent_at):
    n = home.shape[1]
    down = lax.broadcasted_iota(i32, (n, n), 0)
    across = lax.broadcasted_iota(i32, (n, n), 1)
    before = (home_at == home) & sent_at & (down < across)
    return jnp.sum(before.astype(i32), axis=0, keepdims=True)


def dot(a, b):
    return jnp.dot(a, b, preferred_element_type=f32)


def dot_t(a, b):
    return lax.dot_general(a, b, (((1,), (1,)), ((), ())), preferred_element_type=f32)


def pack_kernel(per_home, me_ref, ids_ref, *refs):
    *todo, x_ref, out_ref, to_ref = refs
    slots = out_ref.shape[0]
    width = x_ref.shape[1]
    ids = ids_ref[...]
    n = ids.shape[1]
    ids_at = column(ids)
    home, home_at = ids // per_home, ids_at // per_home
    sent, sent_at = home != me_ref[0], home_at != me_ref[0]
    if todo:
        sent = sent & (todo[0][...] > 0)
        sent_at = sent_at & (column(todo[0][...]) > 0)
    rank = ranks(home, home_at, sent_at)
    to = jnp.where(sent & (rank < room), home * room + rank, -1)
    to_ref[...] = to
    place = (lax.broadcasted_iota(i32, (slots, n), 0) == to).astype(bf16)
    out_ref[:, :width] = dot(place, x_ref[...]).astype(bf16)
    lane = lax.broadcasted_iota(i32, (n, lanes), 1)
    which = (lane == ids_at % per_home).astype(bf16)
    tag = dot(place, which)
    wanted = (lane == home_at + first_count) & sent_at
    counts = jnp.sum(wanted.astype(f32), axis=0, keepdims=True)
    lane = lax.broadcasted_iota(i32, (slots, lanes), 1)
    out_ref[:, width:] = jnp.where(lane >= first_count, counts, tag).astype(bf16)


def left_kernel(per_home, fits, me_ref, ids_ref, count_ref, todo_ref, turns_ref):
    ids = ids_ref[...]
    home = ids // per_home
    away = home != me_ref[0]
    counts = count_ref[...]
    replicas = counts.shape[0]
    sent = jnp.minimum(counts, float(room))
    down = lax.broadcasted_iota(i32, (replicas, replicas), 0)
    across = lax.broadcasted_iota(i32, (replicas, replicas), 1)
    ahead = dot((across < down).astype(bf16), sent.astype(bf16))
    left = counts - jnp.clip(float(fits) - ahead, 0.0, sent)
    lane = lax.broadcasted_iota(i32, (replicas, lanes), 1)
    most = jnp.max(jnp.where(lane >= first_count, left, 0.0)).astype(i32)
    turns_ref[0] = (most + room - 1) // room
    mine = lax.broadcasted_iota(i32, (replicas, lanes), 0) == me_ref[0]
    mine = jnp.sum(jnp.where(mine, ahead, 0.0), axis=0, keepdims=True).astype(i32)
    at = lax.broadcasted_iota(i32, (lanes, home.shape[1]), 0)
    mine = jnp.sum(jnp.where(at == home + first_count, column(mine), 0), axis=0, keepdims=True)
    home_at = column(home)
    rank = ranks(home, home_at, home_at != me_ref[0])
    served = (rank < room) & (mine + rank < fits)
    todo_ref[...] = jnp.where(away & ~served, 1, 0)


def masked_down(x, pick, factors_ref, inner):
    step = 4 * inner
    total = None
    for at in range(0, factors_ref.shape[0], step):
        part = dot_t(x, factors_ref[at : at + step, :]) * pick(at, step)
        part = part[:, : 2 * inner] + part[:, 2 * inner :]
        total = part if total is None else total + part
    return total + pltpu.roll(total, inner, 1)


def fold(both, inner):
    half = both.shape[0] // 2
    lane = lax.broadcasted_iota(i32, (half, 2 * inner), 1)
    return jnp.where(lane < inner, both[:half], both[half:])


def unfold(folded, inner):
    half = folded.shape[0]
    lane = lax.broadcasted_iota(i32, (half, 2 * inner), 1)
    other = pltpu.roll(folded, inner, 1)
    return jnp.concatenate(
        [jnp.where(lane < inner, folded, other), jnp.where(lane < inner, other, folded)], axis=0
    )


def masked_up(both, pick, factors_ref, inner):
    step = 4 * inner
    wide = jnp.concatenate([both, both], axis=1)
    total = None
    for at in range(0, factors_ref.shape[0], step):
        part = dot((wide * pick(at, step)).astype(bf16), factors_ref[at : at + step, :])
        total = part if total is None else total + part
    return total


def picker(onehot, inner):
    width = onehot.shape[1]

    def pick(at, step):
        row = lax.broadcasted_iota(i32, (width, step), 0)
        col = lax.broadcasted_iota(i32, (width, step), 1)
        return dot(onehot, ((col + at) // inner == row).astype(bf16))

    return pick


def own_pick(ids_ref, slot_ref, evict_ref):
    ids = column(ids_ref[...])
    slot = slot_ref[...]
    count = slot.shape[1]
    listed = column(evict_ref[...])
    gone = jnp.max((listed == lax.broadcasted_iota(i32, (listed.shape[0], count), 1)).astype(i32), axis=0, keepdims=True)
    hit = (ids == slot) & (gone == 0)
    hit = jnp.where(hit, 1.0, 0.0)
    return jnp.pad(hit, ((0, 0), (0, lanes - count))).astype(bf16)


def own_down_kernel(inner, ids_ref, slot_ref, evict_ref, x_ref, a_ref, out_ref):
    pick = picker(own_pick(ids_ref, slot_ref, evict_ref), inner)
    out_ref[...] = fold(masked_down(x_ref[...], pick, a_ref, inner), inner).astype(bf16)


def kept_slots(at_ref, held):
    at = at_ref[...]
    return (lax.broadcasted_iota(i32, (held, at.shape[1]), 0) == at).astype(bf16)


def down_kernel(inner, per_home, got_ref, a_ref, *refs):
    own_ref = refs[0] if len(refs) == 7 else None
    out_ref, name_ref, at_ref, count_ref, part_ref, part_sem = refs[-6:]
    slots = got_ref.shape[0]
    width = a_ref.shape[1]
    held = name_ref.shape[0]
    tag = got_ref[:, width:]
    lane = lax.broadcasted_iota(i32, (16, lanes), 1)
    full = dot_t((lane < per_home).astype(bf16), tag)
    down = lax.broadcasted_iota(i32, (slots, slots), 0)
    across = lax.broadcasted_iota(i32, (slots, slots), 1)
    at = dot(full.astype(bf16), (down < across).astype(bf16))
    at_ref[...] = jnp.where(full > 0.5, at, -1.0)[:1].astype(i32)
    keep = kept_slots(at_ref, held)
    x = dot(keep, got_ref[:, :width]).astype(bf16)
    name = dot(keep, tag)
    lane = lax.broadcasted_iota(i32, (held, lanes), 1)
    name = jnp.where(lane < per_home, name, 0.0).astype(bf16)
    name_ref[...] = name
    part_ref[: held // 2, :] = fold(masked_down(x, picker(name, inner), a_ref, inner), inner).astype(bf16)
    if own_ref is not None:
        part_ref[held // 2 :, :] = own_ref[...]
    copies = [
        pltpu.make_async_copy(part_ref, out_ref.at[side], part_sem.at[side])
        for side in range(out_ref.shape[0])
    ]
    for copy in copies:
        copy.start()
    for r in range(count_ref.shape[0]):
        count_ref[r : r + 1, :] = got_ref[r * room : r * room + 1, width:].astype(f32)
    for copy in copies:
        copy.wait()


def low_of(parts_ref, lo, hi, inner):
    total = parts_ref[0, lo:hi, :].astype(f32)
    for k in range(1, parts_ref.shape[0]):
        total = total + parts_ref[k, lo:hi, :].astype(f32)
    return unfold(total.astype(bf16).astype(f32), inner)


def up_kernel(inner, parts_ref, name_ref, at_ref, b_ref, out_ref):
    keep = kept_slots(at_ref, name_ref.shape[0])
    half = name_ref.shape[0] // 2
    both = low_of(parts_ref, 0, half, inner)
    lora = masked_up(both, picker(name_ref[...], inner), b_ref, inner).astype(bf16)
    back = lax.dot_general(keep, lora, (((0,), (0,)), ((), ())), preferred_element_type=f32)
    out_ref[...] = back.astype(bf16)


def own_up_kernel(inner, at, ids_ref, slot_ref, evict_ref, parts_ref, b_ref, out_ref):
    pick = picker(own_pick(ids_ref, slot_ref, evict_ref), inner)
    both = low_of(parts_ref, at, parts_ref.shape[1], inner)
    out_ref[...] = masked_up(both, pick, b_ref, inner)


def base_kernel(steps, side_ref, w_ref, *refs):
    *total, out_ref = refs
    blocks = total[-len(steps) :]
    sum_ = total[0][...] if len(total) > len(steps) else None
    width = blocks[0].shape[1]
    sides = w_ref.shape[0] // width
    for block, step in zip(blocks, steps, strict=True):
        side = lax.rem(side_ref[0] + step, sides)
        weight = w_ref[pl.ds(pl.multiple_of(side * width, width), width), :]
        part = dot(block[...], weight)
        sum_ = part if sum_ is None else sum_ + part
    out_ref[...] = sum_


def came_back(to_ref, back_ref):
    slots = back_ref.shape[0]
    place = (lax.broadcasted_iota(i32, (slots, to_ref.shape[1]), 0) == to_ref[...]).astype(bf16)
    return lax.dot_general(place, back_ref[...], (((0,), (0,)), ((), ())), preferred_element_type=f32)


def last_kernel(to_ref, back_ref, base_ref, own_ref, more_ref, out_ref):
    lora = own_ref[...] + more_ref[...] + came_back(to_ref, back_ref)
    out_ref[...] = (base_ref[...] + adapter_scale * lora).astype(bf16)


def more_kernel(to_ref, todo_ref, back_ref, more_ref, out_ref, left_ref):
    out_ref[...] = more_ref[...] + came_back(to_ref, back_ref)
    left_ref[...] = jnp.where(to_ref[...] >= 0, 0, todo_ref[...])


def swap(blocks, axis):
    return lax.all_to_all(blocks, axis, split_axis=0, concat_axis=0, tiled=True)


def shards(
    x_rows, v_weight, home_a, home_b, cache_a, cache_b, miss_ids, evict_slots, slot_ids, row_ids
):
    n, width = x_rows.shape
    per_home, inner, _ = home_a.shape
    cols = home_b.shape[2]
    replicas = lax.axis_size("replica")
    sides = lax.axis_size("tensor")
    slots = replicas * room
    me = lax.axis_index("replica").astype(i32).reshape(1)
    side = lax.axis_index("tensor").astype(i32).reshape(1)
    ids = row_ids.reshape(1, n)
    a_all = home_a.reshape(per_home * inner, width)
    b_all = home_b.reshape(per_home * inner, cols)

    def send(*todo):
        packed, to = call(
            functools.partial(pack_kernel, per_home),
            (jax.ShapeDtypeStruct((slots, width + lanes), bf16), jax.ShapeDtypeStruct((1, n), i32)),
            me, ids, *todo, x_rows, smem=1, us=3,
        )
        got = swap(packed.reshape(replicas, room, width + lanes), "replica")
        return got.reshape(slots, width + lanes), to

    def down(got, held, *own):
        rows = held // 2 + sum(o.shape[0] for o in own)
        out = (
            jax.ShapeDtypeStruct((sides, rows, lanes), bf16),
            jax.ShapeDtypeStruct((held, lanes), bf16),
            jax.ShapeDtypeStruct((1, slots), i32),
            jax.ShapeDtypeStruct((replicas, lanes), f32),
        )
        return call(
            functools.partial(down_kernel, inner, per_home), out, got, a_all, *own, us=3, hbm_out=1,
            scratch=[pltpu.VMEM((rows, lanes), bf16), pltpu.SemaphoreType.DMA((sides,))],
        )

    def up(parts, name, at):
        return call(
            functools.partial(up_kernel, inner),
            jax.ShapeDtypeStruct((slots, cols), bf16),
            parts, name, at, b_all, us=2,
        )

    def give(back):
        return swap(back.reshape(replicas, room, cols), "replica").reshape(slots, cols)

    got, to = send()
    own = call(
        functools.partial(own_down_kernel, inner),
        jax.ShapeDtypeStruct((n // 2, lanes), bf16),
        ids, slot_ids, evict_slots, x_rows, cache_a.reshape(-1, width), us=3, limit=16 << 20,
    )

    def shift(block, by):
        return lax.ppermute(block, "tensor", [(k, (k + by) % sides) for k in range(sides)])

    def base(total, home_step, blocks):
        steps = tuple(s % sides for s in home_step)
        return call(
            functools.partial(base_kernel, steps), jax.ShapeDtypeStruct((n, cols), f32),
            side, v_weight, *total, *blocks, smem=1,
        )

    near = [shift(x_rows, step) for step in (1, -1, 2, -2)]
    part, name, at, counts = down(got, fits, own)
    part, *near = lax.optimization_barrier((part, *near))
    parts = swap(part, "tensor")
    far = [shift(near[2], 1), shift(near[3], -1), shift(near[2], 2)]
    frozen = base((), (0, -1, 1, -2, 2), (x_rows, *near))
    unserved, turns = call(
        functools.partial(left_kernel, per_home, fits),
        (jax.ShapeDtypeStruct((1, n), i32), jax.ShapeDtypeStruct((1,), i32)),
        me, ids, counts, smem=1, smem_out=1, us=2,
    )
    parts, frozen, unserved, turns = lax.optimization_barrier((parts, frozen, unserved, turns))
    back = give(up(parts, name, at))
    own_lora = call(
        functools.partial(own_up_kernel, inner, fits // 2),
        jax.ShapeDtypeStruct((n, cols), f32),
        ids, slot_ids, evict_slots, parts, cache_b.reshape(-1, cols),
    )
    frozen = base((frozen,), (-3, 3, 4), far)
    unserved, turns, back = lax.optimization_barrier((unserved, turns, back))

    def again(state):
        turn, unserved, more = state
        got, to = send(unserved)
        part, name, at, _ = down(got, slots)
        back = give(up(swap(part, "tensor"), name, at))
        more, unserved = call(
            more_kernel,
            (jax.ShapeDtypeStruct((n, cols), f32), jax.ShapeDtypeStruct((1, n), i32)),
            to, unserved, back, more,
        )
        return turn + 1, unserved, more

    state = (jnp.int32(0), unserved, jnp.zeros((n, cols), f32))
    _, _, more = lax.while_loop(lambda s: s[0] < turns[0], again, state)
    return call(
        last_kernel,
        jax.ShapeDtypeStruct((n, cols), bf16),
        to, back, frozen, own_lora, more,
    )


def solution(mesh):
    return jax.shard_map(
        shards,
        mesh=mesh,
        in_specs=(
            P("replica", "tensor"),
            P(None, "tensor"),
            P("replica", None, "tensor"),
            P("replica", None, "tensor"),
            P("replica", None, "tensor"),
            P("replica", None, "tensor"),
            P("replica", None),
            P("replica", None),
            P("replica", None),
            P("replica"),
        ),
        out_specs=P("replica", "tensor"),
        check_vma=False,
    )
```
